32 devices in a mesh: gx: 8 (over y, x, core), gy: 4 (over z).
Axes of the slice: x: 2, y: 2, z: 4, core: 2. Of those that a mesh axis runs over, the one named last changes fastest.
Arguments:
- velocity: float32 [3, 512, 128, 128], P(None, 'gx', 'gy'), may hold values from -6 to 6
- inflow: float32 [3, 128, 128], P(None, 'gy'), may hold values from -6 to 6
- azimuth: float32 [32], replicated, may hold values from -3.140625 to 3.140625
- positions: int32 [32, 2], replicated, may hold values from 0 to 511, as said below
- crossings: int32 [32, 6], replicated, may hold values from -1 to 95, as said below
- lag_state: float32 [96, 128], P(('gx', 'gy')), may hold values from -0.5 to 1.5
- lag_rate: float32 [96, 128], P(('gx', 'gy')), may hold values from 0.05 to 0.8
- chord_len: float32 [128], replicated, may hold values from 0.3 to 1.5
- twist_angle: float32 [128], replicated, may hold values from -0.4 to 0.4
Outputs:
- velocity_out: float32 [3, 512, 128, 128], P(None, 'gx', 'gy')
- state_out: float32 [96, 128], P(('gx', 'gy'))
The draws below stay inside these ranges and needn't reach their ends.
Inputs may be any that keep to these rules, and one draw needn't show every extreme that they name: `positions`: every rotor's hub lies in the tile of its cell, 2 or more cells from both x edges of that tile and at most 15 cells below its upper y edge; a tile holds at most two hubs, and two hubs in one tile differ in x. `crossings`: row t lists the blades 3 r, 3 r + 1, 3 r + 2 of every rotor r whose hub lies in tile t, then of some of the rotors whose hub lies in the tile just before t along y (cyclic, same x), and -1 in the remaining entries at the end. Every blade appears in one or two rows; some rows hold 6 blades.
All inputs are finite; a program needn't handle non-finite values.
Results may differ from the reference program's by a relative error of at most 0.0003.
Values sent between devices are 32-bit elements; how exact they have to be, the bound alone decides.
A program may use at most 128 MiB of HBM per device.

```python
import math
import jax
import jax.numpy as jnp
from jax import lax

CX = 64
CY = 32
NZ = 128
SEC = 128
RADIUS = 12
HUB = 15
STEPS = 2
CAP = 6
NX = 512
NY = 128
ROTORS = 32
BLADES = 96


def farm_layout(key):
    key = jax.random.fold_in(key, 11)
    k_rot, k_perm, k_x, k_y, k_keep = jax.random.split(key, 5)
    tiles_x = NX // CX
    tiles_y = NY // CY
    tile_total = tiles_x * tiles_y
    pattern_base = jnp.array([2, 0, 2, 0], dtype=jnp.int32)
    pattern = jnp.tile(pattern_base, tiles_y // 4)
    shift_by = jax.random.randint(k_rot, (tiles_x, 1), 0, tiles_y)
    columns = (jnp.arange(tiles_y, dtype=jnp.int32)[None, :] + shift_by) % tiles_y
    tile_counts = pattern[columns].reshape(-1)
    staggered = (columns % 4 == 2).astype(jnp.int32).reshape(-1)
    slot_ends = jnp.cumsum(tile_counts)
    starts = slot_ends - tile_counts
    slot_ids = jnp.arange(ROTORS, dtype=jnp.int32)
    tile_of = jnp.sum((slot_ends[None, :] <= slot_ids[:, None]).astype(jnp.int32), axis=1)
    within = slot_ids - starts[tile_of]
    col_x = tile_of // tiles_y
    row_y = tile_of % tiles_y
    spacing = (CX - 4) // 2
    stagger = (CX - 4) // 4 if CX >= 32 else 0
    jitter_top = max(CX // 32, 2)
    jit_x = jax.random.randint(k_x, (tile_total,), 0, jitter_top)
    jit_y = jax.random.randint(k_y, (ROTORS,), 0, RADIUS + 3)
    hub_x = col_x * CX + 2 + within * spacing + stagger * staggered[tile_of] + jit_x[tile_of]
    hub_y = row_y * CY + CY - RADIUS - 3 + jit_y
    shuffle = jax.random.permutation(k_perm, ROTORS).astype(jnp.int32)
    positions = jnp.zeros((ROTORS, 2), jnp.int32).at[shuffle].set(jnp.stack([hub_x, hub_y], axis=1))
    keep_slot = jax.random.randint(k_keep, (ROTORS,), 0, 2)
    below_row = (jnp.arange(tiles_y, dtype=jnp.int32) - 1) % tiles_y
    below_tile = (jnp.arange(tiles_x, dtype=jnp.int32)[:, None] * tiles_y + below_row[None, :]).reshape(-1)
    pair_index = jnp.arange(2, dtype=jnp.int32)[None, :]
    own_valid = pair_index < tile_counts[:, None]
    own_slot = jnp.clip(starts[:, None] + pair_index, 0, ROTORS - 1)
    low_slot = jnp.clip(starts[below_tile][:, None] + pair_index, 0, ROTORS - 1)
    low_valid = (pair_index < tile_counts[below_tile][:, None]) & (keep_slot[low_slot] == 1)
    cand_slot = jnp.concatenate([own_slot, low_slot], axis=1)
    cand_valid = jnp.concatenate([own_valid, low_valid], axis=1).astype(jnp.int32)
    cand_rank = jnp.cumsum(cand_valid, axis=1) - 1
    places = jnp.arange(CAP // 3, dtype=jnp.int32)
    matches = (cand_valid[:, :, None] == 1) & (cand_rank[:, :, None] == places[None, None, :])
    picked_slot = jnp.sum(jnp.where(matches, cand_slot[:, :, None], 0), axis=1)
    picked_valid = jnp.any(matches, axis=1)
    rotor_pick = shuffle[picked_slot]
    blades = 3 * rotor_pick[:, :, None] + jnp.arange(3, dtype=jnp.int32)[None, None, :]
    listing = jnp.where(picked_valid[:, :, None], blades, -1).reshape(tile_total, CAP)
    return (positions, listing)


def draw_positions(key, part):
    return farm_layout(key)[0]


def draw_crossings(key, part):
    return farm_layout(key)[1]


def levels(own_key, dims, pieces, low, largest):
    def one(axis_at, blocks):
        steps = jax.random.uniform(jax.random.fold_in(jax.random.fold_in(own_key, 6), axis_at), (blocks,), jnp.float32, low / len(pieces), largest / len(pieces))
        return jnp.repeat(jnp.exp(steps), dims[axis_at] // blocks).reshape((-1,) + (1,) * (len(dims) - axis_at - 1))

    gain = one(*pieces[0])
    for cut in pieces[1:]:
        gain = gain * one(*cut)
    return gain


def normal_values(rng, dims, scale, most, shards=(), kind=jnp.bfloat16):
    level = levels(rng, dims, shards, -0.22, 0.18) if shards else 1.0
    entries = jax.random.normal(rng, dims, jnp.float32) * scale * level
    return jnp.minimum(jnp.maximum(entries, -most), most).astype(kind)


def setup_inputs(seed: int = 0) -> dict:
    key_list = jax.random.split(jax.random.key(seed), 10)
    velocity = normal_values(key_list[0], (3, NX, NY, NZ), 1.0, 6.0, ((1, 8), (2, 4)), jnp.float32)
    inflow = normal_values(key_list[1], (3, NY, NZ), 1.0, 6.0, ((1, 4),), jnp.float32)
    azimuth = jnp.clip(jax.random.uniform(key_list[2], (ROTORS,), jnp.float32, -3.140625, 3.140625), -3.140625, 3.140625)
    positions = draw_positions(jax.random.fold_in(key_list[9], 71), 0)
    crossings = draw_crossings(jax.random.fold_in(key_list[9], 71), 0)
    lag_state = jnp.clip(-0.5 + 2.0 * jax.random.uniform(key_list[5], (BLADES, SEC), jnp.float32) ** levels(key_list[5], (BLADES, SEC), ((0, 32),), -0.2, 0.2), -0.5, 1.5)
    lag_rate = jnp.clip(jnp.exp(math.log(0.8) - 2.7725887 * jax.random.uniform(key_list[6], (BLADES, SEC), jnp.float32) ** levels(key_list[6], (BLADES, SEC), ((0, 32),), -0.2, 0.2)), 0.05, 0.8)
    chord_len = jnp.clip(jnp.exp(jax.random.uniform(key_list[7], (SEC,), jnp.float32, math.log(0.3), math.log(1.5))), 0.3, 1.5)
    twist_angle = jnp.clip(jax.random.uniform(key_list[8], (SEC,), jnp.float32, -0.4, 0.4), -0.4, 0.4)
    return {"velocity": velocity, "inflow": inflow, "azimuth": azimuth, "positions": positions, "crossings": crossings, "lag_state": lag_state, "lag_rate": lag_rate, "chord_len": chord_len, "twist_angle": twist_angle}


EPSILON = 2.0
SUPPORT = 3.0
TURN_RATE = 0.1
SPIN = 0.25
LIFT_SLOPE = 2.0 * math.pi
FORCE_SCALE = 0.15
ADVECT = 0.5
DIFFUSE = 0.05
PRECISE = lax.Precision.HIGHEST

def taper_kernel(distance):
    square = distance * distance
    taper_term = jnp.maximum(1.0 - square / (SUPPORT * SUPPORT), 0.0)
    return jnp.exp(-square / (EPSILON * EPSILON)) * taper_term * taper_term / (EPSILON * math.sqrt(math.pi))

def blade_geometry(blade_ids, azimuth, step_id, sections):
    rotor_ids = blade_ids // 3
    azimuths = azimuth[rotor_ids] + TURN_RATE * step_id + 2.0 * math.pi / 3.0 * (blade_ids % 3).astype(jnp.float32)
    radius = RADIUS * (jnp.arange(sections, dtype=jnp.float32) + 0.5) / sections
    return (jnp.cos(azimuths), jnp.sin(azimuths), radius)

def window_kernels(cosines, sine_az, radius, depth_z):
    offsets_y = jnp.arange(2 * RADIUS + 7, dtype=jnp.float32) - (RADIUS + 3)
    heights = jnp.arange(depth_z, dtype=jnp.float32)
    kern_y = taper_kernel(offsets_y[None, None, :] - radius[None, :, None] * sine_az[:, None, None])
    kern_z = taper_kernel(heights[None, None, :] - HUB - radius[None, :, None] * cosines[:, None, None])
    return (kern_y, kern_z)

def blade_forces(samples, lag_now, rates, cosines, sine_az, radius, chord_len, twist_angle):
    cos_b = cosines[:, None]
    sin_b = sine_az[:, None]
    axial_wind = samples[:, 0]
    tangential = SPIN * radius[None, :] - (samples[:, 1] * cos_b - samples[:, 2] * sin_b)
    magnitude = jnp.sqrt(axial_wind * axial_wind + tangential * tangential + 1.0)
    lift_static = LIFT_SLOPE * (axial_wind * jnp.cos(twist_angle) - tangential * jnp.sin(twist_angle)) / magnitude
    updated = lag_now + rates * (lift_static - lag_now)
    lift_force = FORCE_SCALE * chord_len * updated * magnitude
    forces = jnp.stack([-lift_force * tangential, lift_force * axial_wind * cos_b, -lift_force * axial_wind * sin_b], axis=1)
    return (updated, forces)

def advance(velocity, inflow, body_force):

    def advance_one(operands):
        grid_part, inflow_edge, push_part = operands
        x_prev = jnp.concatenate([inflow_edge[None], grid_part[:-1]], axis=0)
        x_next = jnp.concatenate([grid_part[1:], grid_part[-1:]], axis=0)
        y_next = jnp.roll(grid_part, -1, axis=1)
        y_prev = jnp.roll(grid_part, 1, axis=1)
        z_next = jnp.concatenate([grid_part[:, :, 1:], grid_part[:, :, -1:]], axis=2)
        z_prev = jnp.concatenate([jnp.zeros_like(grid_part[:, :, :1]), grid_part[:, :, :-1]], axis=2)
        neighbours = x_prev + x_next + y_next + y_prev + z_next + z_prev
        return grid_part + ADVECT * (x_prev - grid_part) + DIFFUSE * (neighbours - 6.0 * grid_part) + push_part
    return lax.map(advance_one, (velocity, inflow, body_force))

def reference(velocity, inflow, azimuth, positions, crossings, lag_state, lag_rate, chord_len, twist_angle):
    blade_ids = jnp.arange(BLADES, dtype=jnp.int32)
    rotor_ids = blade_ids // 3
    hub_x = positions[rotor_ids, 0]
    hub_y = positions[rotor_ids, 1]
    member = jnp.any(crossings[:, :, None] == blade_ids[None, None, :], axis=1).astype(jnp.float32)
    reach_y = RADIUS + 3
    offsets_x = jnp.arange(5, dtype=jnp.int32) - 2
    offsets_y = jnp.arange(2 * reach_y + 1, dtype=jnp.int32) - reach_y
    kern_x = taper_kernel(offsets_x.astype(jnp.float32))
    lag_now = lag_state
    for step_id in range(STEPS):
        cosines, sine_az, radius = blade_geometry(blade_ids, azimuth, step_id, SEC)
        kern_y, kern_z = window_kernels(cosines, sine_az, radius, NZ)

        def locate(blade_id):
            cells_x = hub_x[blade_id] + offsets_x
            cells_y = (hub_y[blade_id] + offsets_y) % NY
            tile_ids = hub_x[blade_id] // CX * (NY // CY) + cells_y // CY
            return (cells_x, cells_y, member[tile_ids, blade_id])

        def sample_one(blade_id):
            cells_x, cells_y, member_mask = locate(blade_id)
            window = velocity[:, cells_x[:, None], cells_y[None, :], :]
            flattened = jnp.einsum('i,cijz->cjz', kern_x, window, precision=PRECISE) * member_mask[None, :, None]
            inner_sum = jnp.dot(flattened.reshape(-1, NZ), kern_z[blade_id].T, precision=PRECISE).reshape(3, -1, SEC)
            return lax.optimization_barrier(jnp.sum(inner_sum * kern_y[blade_id].T[None], axis=1))
        samples = lax.map(sample_one, blade_ids)
        lag_now, forces = blade_forces(samples, lag_now, lag_rate, cosines, sine_az, radius, chord_len, twist_angle)

        def spread_one(force_field, blade_id):
            cells_x, cells_y, member_mask = locate(blade_id)
            weighted = forces[blade_id][:, None, :] * kern_y[blade_id].T[None]
            spread = jnp.dot(weighted.reshape(-1, SEC), kern_z[blade_id], precision=PRECISE).reshape(3, -1, NZ)
            spread = spread * member_mask[None, :, None]
            block_add = kern_x[None, :, None, None] * spread[:, None]
            return (force_field.at[:, cells_x[:, None], cells_y[None, :], :].add(block_add), None)
        body_force, _ = lax.scan(spread_one, jnp.zeros_like(velocity), blade_ids)
        velocity = advance(velocity, inflow, body_force)
    return (velocity, lag_now)
```

```python
import functools
import math

import jax
import jax.numpy as jnp
from jax import lax
from jax.experimental import pallas as pl
from jax.experimental.pallas import tpu as pltpu
from jax.sharding import PartitionSpec as P

RADIUS = 12
HUB = 15
STEPS = 2
EPSILON = 2.0
SUPPORT = 3.0
TURN_RATE = 0.1
SPIN = 0.25
LIFT_SLOPE = 2.0 * math.pi
FORCE_SCALE = 0.15
ADVECT = 0.5
DIFFUSE = 0.05
PRECISE = lax.Precision.HIGHEST
MESH = pl.DeviceIdType.MESH
BLADES = 3
ENTRIES = 2
ROWS = 8
CHUNKS = 4


def taper_const(distance):
    square = distance * distance
    term = max(1.0 - square / (SUPPORT * SUPPORT), 0.0)
    return math.exp(-square / EPSILON**2) * term * term / (EPSILON * math.sqrt(math.pi))


KERN_X = [taper_const(float(i)) for i in range(3)]


def taper_kernel(distance):
    square = distance * distance
    term = jnp.maximum(1.0 - square * (1.0 / (SUPPORT * SUPPORT)), 0.0)
    return (
        jnp.exp(square * (-1.0 / (EPSILON * EPSILON)))
        * (term * term)
        * (1.0 / (EPSILON * math.sqrt(math.pi)))
    )


def weight_x(offset):
    dist = jnp.abs(offset)
    return jnp.where(
        dist == 0,
        KERN_X[0],
        jnp.where(dist == 1, KERN_X[1], jnp.where(dist == 2, KERN_X[2], 0.0)),
    ).astype(jnp.float32)


def farm_kernel(
    nx,
    ny,
    vel_hbm,
    inflow_ref,
    az_ref,
    pos_ref,
    cross_ref,
    lag_ref,
    rate_ref,
    chord_ref,
    twist_ref,
    out_hbm,
    state_ref,
    grid0,
    grid1,
    grid2,
    halo_x,
    halo_y,
    face_y,
    part_out,
    part_in,
    kern_y,
    kern_z,
    spread,
    lag_pack,
    lag_g1,
    lag_g2,
    end_pack,
    end_g1,
    end_g2,
    load_sem,
    store_sem,
    hx_send,
    hx_recv,
    hy_send,
    hy_recv,
    ps_send,
    ps_recv,
    gy_send,
    gy_recv,
    gx_send,
    gx_recv,
):
    grids = (grid0, grid1, grid2)
    _, cx2, cy, nz = grid0.shape
    cx = cx2 - 2
    total_y = cy * ny
    gx = lax.axis_index("gx")
    gy = lax.axis_index("gy")
    tile = gx * ny + gy
    east = lax.rem(gx + 1, nx)
    west = lax.rem(gx + nx - 1, nx)
    up = lax.rem(gy + 1, ny)
    down = lax.rem(gy + ny - 1, ny)

    load = pltpu.make_async_copy(vel_hbm, grid0.at[:, pl.ds(1, cx)], load_sem)
    load.start()

    barrier = pltpu.get_barrier_semaphore()
    for d in range(1, ny):
        pl.semaphore_signal(
            barrier, inc=1, device_id={"gy": lax.rem(gy + d, ny)}, device_id_type=MESH
        )
    for d in range(1, nx):
        pl.semaphore_signal(
            barrier, inc=1, device_id={"gx": lax.rem(gx + d, nx)}, device_id_type=MESH
        )

    rotor, hub_x, load_x, shift_y, valid, az = [], [], [], [], [], []
    for e in range(ENTRIES):
        blade = cross_ref[BLADES * e, tile]
        r = jnp.where(blade >= 0, blade, 0) // BLADES
        rotor.append(jnp.where(blade >= 0, r, -1))
        valid.append(jnp.where(blade >= 0, 1.0, 0.0).astype(jnp.float32))
        hub_x.append(jnp.where(blade >= 0, pos_ref[0, r] - gx * cx, 2))
        load_x.append(jnp.clip(hub_x[e], 2, cx - 3))
        off = gy * cy - pos_ref[1, r] + total_y + total_y // 2
        shift_y.append(lax.rem(off, total_y) - total_y // 2)
        az.append(az_ref[r])

    def matches(other):
        found = []
        for f in range(ENTRIES):
            blade = cross_ref[BLADES * f, other]
            found.append(jnp.where(blade >= 0, jnp.where(blade >= 0, blade, 0) // BLADES, -2))
        return [
            [jnp.where(rotor[e] == found[f], 1.0, 0.0).astype(jnp.float32) for f in range(ENTRIES)]
            for e in range(ENTRIES)
        ]

    row = lax.broadcasted_iota(jnp.int32, (ROWS, nz), 0)
    first = row < BLADES
    lane8 = lax.broadcasted_iota(jnp.int32, (ROWS, nz), 1).astype(jnp.float32)
    radius = RADIUS * (lane8 + 0.5) / nz
    spin = jnp.where(first, row, row - BLADES).astype(jnp.float32) * (2.0 * math.pi / 3.0)
    base = jnp.where(first, az[0], az[1])
    mask_rows = []
    for other in (gx * ny + down, gx * ny + up):
        m = matches(other)
        mask_rows.append(
            (jnp.where(first, m[0][0], m[1][1]), jnp.where(first, m[0][1], m[1][0]))
        )
    cos_all, sin_all = [], []
    rows_y = lax.broadcasted_iota(jnp.int32, (cy, nz), 0)
    rows_z = lax.broadcasted_iota(jnp.int32, (nz, nz), 0).astype(jnp.float32) - HUB
    for n in range(STEPS):
        theta = base + TURN_RATE * n + spin
        cos_n, sin_n = jnp.cos(theta), jnp.sin(theta)
        cos_all.append(cos_n)
        sin_all.append(sin_n)
        rc, rs = radius * cos_n, radius * sin_n
        for e in range(ENTRIES):
            y_rel = (rows_y + shift_y[e]).astype(jnp.float32)
            for b in range(BLADES):
                i = BLADES * e + b
                kern_y[n, e, :, b * nz : (b + 1) * nz] = taper_kernel(y_rel - rs[i : i + 1]) * valid[e]
                kern_z[n, e, :, b * nz : (b + 1) * nz] = taper_kernel(rows_z - rc[i : i + 1])
    cos_t, sin_t = jnp.cos(twist_ref[...]), jnp.sin(twist_ref[...])
    chord = FORCE_SCALE * chord_ref[...]

    lag_pack[0:BLADES] = lag_ref[...]
    lag_pack[BLADES : 2 * BLADES] = rate_ref[...]
    lag_pack[2 * BLADES : ROWS] = jnp.zeros((ROWS - 2 * BLADES, nz), jnp.float32)

    pl.semaphore_wait(barrier, nx - 1 + ny - 1)

    started = []

    def send(src, dst, send_sem, recv_sem, axis, peer):
        copy = pltpu.make_async_remote_copy(
            src_ref=src,
            dst_ref=dst,
            send_sem=send_sem,
            recv_sem=recv_sem,
            device_id={axis: peer},
            device_id_type=MESH,
        )
        copy.start()
        started.append(copy)
        return copy

    def gather_start(k, pack, first_level):
        copies = [
            send(pack, first_level.at[gy], gy_send.at[k, d], gy_recv.at[k, d], "gy", lax.rem(gy + d, ny))
            for d in range(1, ny)
        ]
        first_level[gy] = pack[...]
        return copies

    def gather_next(k, copies, first_level, second_level):
        for copy in copies:
            copy.wait_recv()
        copies = [
            send(first_level, second_level.at[gx], gx_send.at[k, d], gx_recv.at[k, d], "gx", lax.rem(gx + d, nx))
            for d in range(1, nx)
        ]
        second_level[gx] = first_level[...]
        return copies

    lag_copies = gather_start(0, lag_pack, lag_g1)
    load.wait()

    lag = None
    rate = None
    zero_rows = jnp.zeros((ROWS - 2 * BLADES, nz), jnp.float32)
    lane = lax.broadcasted_iota(jnp.int32, (cy, nz), 1)
    row_c = lax.broadcasted_iota(jnp.int32, (cy, nz), 0)
    is_first_z, is_last_z = lane == 0, lane == nz - 1
    is_first_y, is_last_y = row_c == 0, row_c == cy - 1
    end_copies = None
    stores = []
    for n in range(STEPS):
        src, dst = grids[n], grids[n + 1]
        halo_copies = [
            send(src.at[:, cx], halo_x.at[n, 0], hx_send.at[n, 0], hx_recv.at[n, 0], "gx", east),
            send(src.at[:, 1], halo_x.at[n, 1], hx_send.at[n, 1], hx_recv.at[n, 1], "gx", west),
        ]
        flat = src.reshape(3 * cx2 * cy, nz)
        for c in range(3):
            start = (c * cx2 + 1) * cy
            face_y[n, 0, c] = flat[pl.ds(start + cy - 1, cx, stride=cy), :]
            face_y[n, 1, c] = flat[pl.ds(start, cx, stride=cy), :]
        halo_copies += [
            send(face_y.at[n, 0], halo_y.at[n, 0], hy_send.at[n, 0], hy_recv.at[n, 0], "gy", up),
            send(face_y.at[n, 1], halo_y.at[n, 1], hy_send.at[n, 1], hy_recv.at[n, 1], "gy", down),
        ]

        sampled = [[], [], []]
        for e in range(ENTRIES):
            field = None
            for i in range(-2, 3):
                term = KERN_X[abs(i)] * src[:, load_x[e] + 1 + i]
                field = term if field is None else field + term
            inner = jnp.dot(
                field.reshape(3 * cy, nz),
                kern_z[n, e],
                precision=PRECISE,
                preferred_element_type=jnp.float32,
            )
            for c in range(3):
                reduced = jnp.sum(inner[c * cy : (c + 1) * cy] * kern_y[n, e], axis=0, keepdims=True)
                sampled[c] += [reduced[:, b * nz : (b + 1) * nz] for b in range(BLADES)]
        for c in range(3):
            part_out[n, c] = jnp.concatenate(sampled[c] + [zero_rows], axis=0)
        part_copies = [
            send(part_out.at[n], part_in.at[n, 0], ps_send.at[n, 0], ps_recv.at[n, 0], "gy", up),
            send(part_out.at[n], part_in.at[n, 1], ps_send.at[n, 1], ps_recv.at[n, 1], "gy", down),
        ]
        if n == 0:
            lag_copies = gather_next(0, lag_copies, lag_g1, lag_g2)

        for copy in halo_copies:
            copy.wait_recv()
        src[:, 0] = jnp.where(gx == 0, inflow_ref[...], halo_x[n, 0])
        src[:, cx + 1] = jnp.where(gx == nx - 1, src[:, cx], halo_x[n, 1])

        def plane(x, carry):
            for c in range(3):
                cur = src[c, x + 1]
                y_prev = jnp.where(is_first_y, halo_y[n, 0, c, pl.ds(x, 1), :], pltpu.roll(cur, 1, 0))
                y_next = jnp.where(is_last_y, halo_y[n, 1, c, pl.ds(x, 1), :], pltpu.roll(cur, cy - 1, 0))
                z_prev = jnp.where(is_first_z, 0.0, pltpu.roll(cur, 1, 1))
                z_next = jnp.where(is_last_z, cur, pltpu.roll(cur, nz - 1, 1))
                others = src[c, x + 2] + y_prev + y_next + z_prev + z_next
                dst[c, x + 1] = (
                    (1.0 - ADVECT - 6.0 * DIFFUSE) * cur
                    + (ADVECT + DIFFUSE) * src[c, x]
                    + DIFFUSE * others
                )
            return carry

        lax.fori_loop(0, cx, plane, 0)

        for copy in part_copies:
            copy.wait_recv()
        whole = []
        for c in range(3):
            total = part_out[n, c]
            for side in range(2):
                other = part_in[n, side, c]
                same, cross = mask_rows[side]
                swapped = jnp.where(first, pltpu.roll(other, ROWS - BLADES, 0), pltpu.roll(other, BLADES, 0))
                total = total + (same * other + cross * swapped)
            whole.append(total)
        if n == 0:
            for copy in lag_copies:
                copy.wait_recv()
            state_rows, rate_rows = [], []
            for e in range(ENTRIES):
                r = jnp.maximum(rotor[e], 0)
                block = lag_g2[r // ny, lax.rem(r, ny)]
                state_rows.append(block[0:BLADES])
                rate_rows.append(block[BLADES : 2 * BLADES])
            lag = jnp.concatenate(state_rows + [zero_rows], axis=0)
            rate = jnp.concatenate(rate_rows + [zero_rows], axis=0)
        cos_b, sin_b = cos_all[n], sin_all[n]
        axial = whole[0]
        tangential = SPIN * radius - (whole[1] * cos_b - whole[2] * sin_b)
        magnitude = jnp.sqrt(axial * axial + tangential * tangential + 1.0)
        lift_static = LIFT_SLOPE * (axial * cos_t - tangential * sin_t) / magnitude
        lag = lag + rate * (lift_static - lag)
        if n == STEPS - 1:
            end_pack[...] = lag
            end_copies = gather_start(1, end_pack, end_g1)
        lift = chord * lag * magnitude
        forces = (-lift * tangential, lift * axial * cos_b, -lift * axial * sin_b)
        for e in range(ENTRIES):
            weighted = []
            for c in range(3):
                weighted.append(
                    jnp.concatenate(
                        [
                            forces[c][BLADES * e + b : BLADES * e + b + 1]
                            * kern_y[n, e, :, b * nz : (b + 1) * nz]
                            for b in range(BLADES)
                        ],
                        axis=1,
                    )
                )
            pushed = lax.dot_general(
                jnp.concatenate(weighted, axis=0),
                kern_z[n, e],
                (((1,), (1,)), ((), ())),
                precision=PRECISE,
                preferred_element_type=jnp.float32,
            )
            spread[n, e] = pushed.reshape(3, cy, nz)
        if n == STEPS - 1:
            end_copies = gather_next(1, end_copies, end_g1, end_g2)

        def push(x, carry):
            w0, w1 = weight_x(x - hub_x[0]), weight_x(x - hub_x[1])
            for c in range(3):
                dst[c, x + 1] = dst[c, x + 1] + (w0 * spread[n, 0, c] + w1 * spread[n, 1, c])
            return carry

        if n < STEPS - 1:
            lax.fori_loop(0, cx, push, 0)
        else:
            size = cx // CHUNKS
            for k in range(CHUNKS):
                lax.fori_loop(k * size, (k + 1) * size, push, 0)
                store = pltpu.make_async_copy(
                    dst.at[:, pl.ds(1 + k * size, size)],
                    out_hbm.at[:, pl.ds(k * size, size)],
                    store_sem.at[k],
                )
                store.start()
                stores.append(store)

    for copy in end_copies:
        copy.wait_recv()
    home_x = pos_ref[0, tile] // cx
    home_y = pos_ref[1, tile] // cy
    block = end_g2[home_x, home_y]
    in_first = cross_ref[0, home_x * ny + home_y] == BLADES * tile
    state_ref[...] = jnp.where(in_first, block[0:BLADES], block[BLADES : 2 * BLADES])
    for copy in started:
        copy.wait_send()
    for store in stores:
        store.wait()


def per_device(
    velocity, inflow, azimuth, positions, crossings, lag_state, lag_rate, chord_len, twist_angle
):
    nx = lax.axis_size("gx")
    ny = lax.axis_size("gy")
    comps, cx, cy, nz = velocity.shape
    own, sections = lag_state.shape
    assert comps == 3 and own == BLADES and sections == nz
    f32 = jnp.float32
    grid = pltpu.VMEM((3, cx + 2, cy, nz), f32)
    dma = pltpu.SemaphoreType.DMA
    vmem = pl.BlockSpec(memory_space=pltpu.VMEM)
    smem = pl.BlockSpec(memory_space=pltpu.SMEM)
    hbm = pl.BlockSpec(memory_space=pl.ANY)
    return pl.pallas_call(
        functools.partial(farm_kernel, nx, ny),
        out_shape=(
            jax.ShapeDtypeStruct(velocity.shape, f32),
            jax.ShapeDtypeStruct(lag_state.shape, f32),
        ),
        in_specs=[hbm, vmem, smem, smem, smem, vmem, vmem, vmem, vmem],
        out_specs=(hbm, vmem),
        scratch_shapes=[
            grid,
            grid,
            grid,
            pltpu.VMEM((STEPS, 2, 3, cy, nz), f32),
            pltpu.VMEM((STEPS, 2, 3, cx, nz), f32),
            pltpu.VMEM((STEPS, 2, 3, cx, nz), f32),
            pltpu.VMEM((STEPS, 3, ROWS, nz), f32),
            pltpu.VMEM((STEPS, 2, 3, ROWS, nz), f32),
            pltpu.VMEM((STEPS, ENTRIES, cy, BLADES * nz), f32),
            pltpu.VMEM((STEPS, ENTRIES, nz, BLADES * nz), f32),
            pltpu.VMEM((STEPS, ENTRIES, 3, cy, nz), f32),
            pltpu.VMEM((ROWS, nz), f32),
            pltpu.VMEM((ny, ROWS, nz), f32),
            pltpu.VMEM((nx, ny, ROWS, nz), f32),
            pltpu.VMEM((ROWS, nz), f32),
            pltpu.VMEM((ny, ROWS, nz), f32),
            pltpu.VMEM((nx, ny, ROWS, nz), f32),
            dma,
            dma((CHUNKS,)),
            dma((STEPS, 2)),
            dma((STEPS, 2)),
            dma((STEPS, 2)),
            dma((STEPS, 2)),
            dma((STEPS, 2)),
            dma((STEPS, 2)),
            dma((2, ny)),
            dma((2, ny)),
            dma((2, nx)),
            dma((2, nx)),
        ],
        compiler_params=pltpu.CompilerParams(
            collective_id=0, has_side_effects=True, vmem_limit_bytes=60 * 1024 * 1024
        ),
        cost_estimate=pl.CostEstimate(
            flops=50_000_000, bytes_accessed=8 * velocity.size, transcendentals=500_000
        ),
    )(
        velocity,
        inflow,
        azimuth,
        positions.T,
        crossings.T,
        lag_state,
        lag_rate,
        chord_len.reshape(1, sections),
        twist_angle.reshape(1, sections),
    )


def solution(mesh):
    return jax.shard_map(
        per_device,
        mesh=mesh,
        in_specs=(
            P(None, "gx", "gy", None),
            P(None, "gy", None),
            P(),
            P(),
            P(),
            P(("gx", "gy"), None),
            P(("gx", "gy"), None),
            P(),
            P(),
        ),
        out_specs=(P(None, "gx", "gy", None), P(("gx", "gy"), None)),
        check_vma=False,
    )
```

```python
import functools
import math

import jax
import jax.numpy as jnp
from jax import lax
from jax.experimental import pallas as pl
from jax.experimental.pallas import tpu as pltpu
from jax.sharding import PartitionSpec as P

RADIUS = 12
HUB = 15
STEPS = 2
EPSILON = 2.0
SUPPORT = 3.0
TURN_RATE = 0.1
SPIN = 0.25
LIFT_SLOPE = 2.0 * math.pi
FORCE_SCALE = 0.15
ADVECT = 0.5
DIFFUSE = 0.05
PRECISE = lax.Precision.HIGHEST
MESH = pl.DeviceIdType.MESH
BLADES = 3
ENTRIES = 2
ROWS = 8
CHUNKS = 3
UNROLL = 4


def taper_const(distance):
    square = distance * distance
    term = max(1.0 - square / (SUPPORT * SUPPORT), 0.0)
    return math.exp(-square / EPSILON**2) * term * term / (EPSILON * math.sqrt(math.pi))


KERN_X = [taper_const(float(i)) for i in range(3)]


def taper_kernel(distance):
    square = distance * distance
    term = jnp.maximum(1.0 - square * (1.0 / (SUPPORT * SUPPORT)), 0.0)
    return (
        jnp.exp(square * (-1.0 / (EPSILON * EPSILON)))
        * (term * term)
        * (1.0 / (EPSILON * math.sqrt(math.pi)))
    )


def weight_x(offset):
    dist = jnp.abs(offset)
    return jnp.where(
        dist == 0,
        KERN_X[0],
        jnp.where(dist == 1, KERN_X[1], jnp.where(dist == 2, KERN_X[2], 0.0)),
    ).astype(jnp.float32)


def farm_kernel(
    nx,
    ny,
    vel_hbm,
    inflow_ref,
    az_ref,
    pos_ref,
    cross_ref,
    lag_ref,
    rate_ref,
    chord_ref,
    twist_ref,
    out_hbm,
    state_ref,
    grid0,
    grid1,
    grid2,
    halo_x,
    halo_y,
    face_y,
    part_out,
    part_in,
    kern_y,
    kern_z,
    spread,
    lag_pack,
    lag_g1,
    lag_g2,
    end_pack,
    end_g1,
    end_g2,
    load_sem,
    store_sem,
    hx_send,
    hx_recv,
    hy_send,
    hy_recv,
    ps_send,
    ps_recv,
    gy_send,
    gy_recv,
    gx_send,
    gx_recv,
):
    grids = (grid0, grid1, grid2)
    _, cx2, cy, nz = grid0.shape
    cx = cx2 - 2
    split = cx // 2
    total_y = cy * ny
    gx = lax.axis_index("gx")
    gy = lax.axis_index("gy")
    tile = gx * ny + gy
    east = lax.rem(gx + 1, nx)
    west = lax.rem(gx + nx - 1, nx)
    up = lax.rem(gy + 1, ny)
    down = lax.rem(gy + ny - 1, ny)

    load = pltpu.make_async_copy(vel_hbm, grid0.at[:, pl.ds(1, cx)], load_sem)
    load.start()

    barrier = pltpu.get_barrier_semaphore()
    for d in range(1, ny):
        pl.semaphore_signal(
            barrier, inc=1, device_id={"gy": lax.rem(gy + d, ny)}, device_id_type=MESH
        )
    for d in range(1, nx):
        pl.semaphore_signal(
            barrier, inc=1, device_id={"gx": lax.rem(gx + d, nx)}, device_id_type=MESH
        )

    rotor, hub_x, load_x, shift_y, valid, az = [], [], [], [], [], []
    for e in range(ENTRIES):
        blade = cross_ref[BLADES * e, tile]
        r = jnp.where(blade >= 0, blade, 0) // BLADES
        rotor.append(jnp.where(blade >= 0, r, -1))
        valid.append(jnp.where(blade >= 0, 1.0, 0.0).astype(jnp.float32))
        hub_x.append(jnp.where(blade >= 0, pos_ref[0, r] - gx * cx, 2))
        load_x.append(jnp.clip(hub_x[e], 2, cx - 3))
        off = gy * cy - pos_ref[1, r] + total_y + total_y // 2
        shift_y.append(lax.rem(off, total_y) - total_y // 2)
        az.append(az_ref[r])

    def matches(other):
        found = []
        for f in range(ENTRIES):
            blade = cross_ref[BLADES * f, other]
            found.append(jnp.where(blade >= 0, jnp.where(blade >= 0, blade, 0) // BLADES, -2))
        return [
            [jnp.where(rotor[e] == found[f], 1.0, 0.0).astype(jnp.float32) for f in range(ENTRIES)]
            for e in range(ENTRIES)
        ]

    row = lax.broadcasted_iota(jnp.int32, (ROWS, nz), 0)
    first = row < BLADES
    lane8 = lax.broadcasted_iota(jnp.int32, (ROWS, nz), 1).astype(jnp.float32)
    radius = RADIUS * (lane8 + 0.5) / nz
    spin = jnp.where(first, row, row - BLADES).astype(jnp.float32) * (2.0 * math.pi / 3.0)
    base = jnp.where(first, az[0], az[1])
    mask_rows = []
    for other in (gx * ny + down, gx * ny + up):
        m = matches(other)
        mask_rows.append(
            (jnp.where(first, m[0][0], m[1][1]), jnp.where(first, m[0][1], m[1][0]))
        )
    cos_all, sin_all = [], []
    rows_y = lax.broadcasted_iota(jnp.int32, (cy, nz), 0)
    rows_z = lax.broadcasted_iota(jnp.int32, (nz, nz), 0).astype(jnp.float32) - HUB
    for n in range(STEPS):
        theta = base + TURN_RATE * n + spin
        cos_n, sin_n = jnp.cos(theta), jnp.sin(theta)
        cos_all.append(cos_n)
        sin_all.append(sin_n)
        rc, rs = radius * cos_n, radius * sin_n
        for e in range(ENTRIES):
            y_rel = (rows_y + shift_y[e]).astype(jnp.float32)
            for b in range(BLADES):
                i = BLADES * e + b
                kern_y[n, e, :, b * nz : (b + 1) * nz] = taper_kernel(y_rel - rs[i : i + 1]) * valid[e]
                kern_z[n, e, :, b * nz : (b + 1) * nz] = taper_kernel(rows_z - rc[i : i + 1])
    cos_t, sin_t = jnp.cos(twist_ref[...]), jnp.sin(twist_ref[...])
    chord = FORCE_SCALE * chord_ref[...]

    lag_pack[0:BLADES] = lag_ref[...]
    lag_pack[BLADES : 2 * BLADES] = rate_ref[...]
    lag_pack[2 * BLADES : ROWS] = jnp.zeros((ROWS - 2 * BLADES, nz), jnp.float32)

    pl.semaphore_wait(barrier, nx - 1 + ny - 1)

    started = []

    def send(src, dst, send_sem, recv_sem, axis, peer):
        copy = pltpu.make_async_remote_copy(
            src_ref=src,
            dst_ref=dst,
            send_sem=send_sem,
            recv_sem=recv_sem,
            device_id={axis: peer},
            device_id_type=MESH,
        )
        copy.start()
        started.append(copy)
        return copy

    def gather_start(k, pack, first_level):
        copies = [
            send(pack, first_level.at[gy], gy_send.at[k, d], gy_recv.at[k, d], "gy", lax.rem(gy + d, ny))
            for d in range(1, ny)
        ]
        first_level[gy] = pack[...]
        return copies

    def gather_next(k, copies, first_level, second_level):
        for copy in copies:
            copy.wait_recv()
        copies = [
            send(first_level, second_level.at[gx], gx_send.at[k, d], gx_recv.at[k, d], "gx", lax.rem(gx + d, nx))
            for d in range(1, nx)
        ]
        second_level[gx] = first_level[...]
        return copies

    lag_copies = gather_start(0, lag_pack, lag_g1)
    load.wait()

    lag = None
    rate = None
    zero_rows = jnp.zeros((ROWS - 2 * BLADES, nz), jnp.float32)
    lane = lax.broadcasted_iota(jnp.int32, (cy, nz), 1)
    row_c = lax.broadcasted_iota(jnp.int32, (cy, nz), 0)
    is_first_z, is_last_z = lane == 0, lane == nz - 1
    is_first_y, is_last_y = row_c == 0, row_c == cy - 1
    end_copies = None
    stores = []
    for n in range(STEPS):
        src, dst = grids[n], grids[n + 1]
        halo_copies = [
            send(src.at[:, cx], halo_x.at[n, 0], hx_send.at[n, 0], hx_recv.at[n, 0], "gx", east),
            send(src.at[:, 1], halo_x.at[n, 1], hx_send.at[n, 1], hx_recv.at[n, 1], "gx", west),
        ]

        sampled = [[], [], []]
        for e in range(ENTRIES):
            field = None
            for i in range(-2, 3):
                term = KERN_X[abs(i)] * src[:, load_x[e] + 1 + i]
                field = term if field is None else field + term
            inner = jnp.dot(
                field.reshape(3 * cy, nz),
                kern_z[n, e],
                precision=PRECISE,
                preferred_element_type=jnp.float32,
            )
            for c in range(3):
                reduced = jnp.sum(inner[c * cy : (c + 1) * cy] * kern_y[n, e], axis=0, keepdims=True)
                sampled[c] += [reduced[:, b * nz : (b + 1) * nz] for b in range(BLADES)]
        for c in range(3):
            part_out[n, c] = jnp.concatenate(sampled[c] + [zero_rows], axis=0)
        part_copies = [
            send(part_out.at[n], part_in.at[n, 0], ps_send.at[n, 0], ps_recv.at[n, 0], "gy", up),
            send(part_out.at[n], part_in.at[n, 1], ps_send.at[n, 1], ps_recv.at[n, 1], "gy", down),
        ]
        flat = src.reshape(3 * cx2 * cy, nz)
        for c in range(3):
            start = (c * cx2 + 1) * cy
            face_y[n, 0, c] = flat[pl.ds(start + cy - 1, cx, stride=cy), :]
            face_y[n, 1, c] = flat[pl.ds(start, cx, stride=cy), :]
        halo_copies += [
            send(face_y.at[n, 0], halo_y.at[n, 0], hy_send.at[n, 0], hy_recv.at[n, 0], "gy", up),
            send(face_y.at[n, 1], halo_y.at[n, 1], hy_send.at[n, 1], hy_recv.at[n, 1], "gy", down),
        ]
        if n == 0:
            lag_copies = gather_next(0, lag_copies, lag_g1, lag_g2)

        def halo_rows(c, x):
            return halo_y[n, 0, c, pl.ds(x, 1), :], halo_y[n, 1, c, pl.ds(x, 1), :]

        def moved(c, x, below, above):
            cur = src[c, x + 1]
            y_prev = jnp.where(is_first_y, below, pltpu.roll(cur, 1, 0))
            y_next = jnp.where(is_last_y, above, pltpu.roll(cur, cy - 1, 0))
            z_prev = jnp.where(is_first_z, 0.0, pltpu.roll(cur, 1, 1))
            z_next = jnp.where(is_last_z, cur, pltpu.roll(cur, nz - 1, 1))
            others = (src[c, x + 2] + (y_prev + y_next)) + (z_prev + z_next)
            return (
                (1.0 - ADVECT - 6.0 * DIFFUSE) * cur
                + (ADVECT + DIFFUSE) * src[c, x]
                + DIFFUSE * others
            )

        def plane_alone(x, carry):
            for c in range(3):
                dst[c, x + 1] = moved(c, x, 0.0, 0.0)
            return carry

        lax.fori_loop(1, split, plane_alone, 0, unroll=UNROLL)

        for copy in part_copies:
            copy.wait_recv()
        whole = []
        for c in range(3):
            total = part_out[n, c]
            for side in range(2):
                other = part_in[n, side, c]
                same, cross = mask_rows[side]
                swapped = jnp.where(first, pltpu.roll(other, ROWS - BLADES, 0), pltpu.roll(other, BLADES, 0))
                total = total + (same * other + cross * swapped)
            whole.append(total)
        if n == 0:
            for copy in lag_copies:
                copy.wait_recv()
            state_rows, rate_rows = [], []
            for e in range(ENTRIES):
                r = jnp.maximum(rotor[e], 0)
                block = lag_g2[r // ny, lax.rem(r, ny)]
                state_rows.append(block[0:BLADES])
                rate_rows.append(block[BLADES : 2 * BLADES])
            lag = jnp.concatenate(state_rows + [zero_rows], axis=0)
            rate = jnp.concatenate(rate_rows + [zero_rows], axis=0)
        cos_b, sin_b = cos_all[n], sin_all[n]
        axial = whole[0]
        tangential = SPIN * radius - (whole[1] * cos_b - whole[2] * sin_b)
        magnitude = jnp.sqrt(axial * axial + tangential * tangential + 1.0)
        lift_static = LIFT_SLOPE * (axial * cos_t - tangential * sin_t) / magnitude
        lag = lag + rate * (lift_static - lag)
        if n == STEPS - 1:
            end_pack[...] = lag
            end_copies = gather_start(1, end_pack, end_g1)
        lift = chord * lag * magnitude
        forces = (-lift * tangential, lift * axial * cos_b, -lift * axial * sin_b)
        for e in range(ENTRIES):
            weighted = []
            for c in range(3):
                weighted.append(
                    jnp.concatenate(
                        [
                            forces[c][BLADES * e + b : BLADES * e + b + 1]
                            * kern_y[n, e, :, b * nz : (b + 1) * nz]
                            for b in range(BLADES)
                        ],
                        axis=1,
                    )
                )
            pushed = lax.dot_general(
                jnp.concatenate(weighted, axis=0),
                kern_z[n, e],
                (((1,), (1,)), ((), ())),
                precision=PRECISE,
                preferred_element_type=jnp.float32,
            )
            spread[n, e] = pushed.reshape(3, cy, nz)
        for copy in halo_copies:
            copy.wait_recv()
        src[:, 0] = jnp.where(gx == 0, inflow_ref[...], halo_x[n, 0])
        src[:, cx + 1] = jnp.where(gx == nx - 1, src[:, cx], halo_x[n, 1])

        def body_force(c, x):
            w0, w1 = weight_x(x - hub_x[0]), weight_x(x - hub_x[1])
            return w0 * spread[n, 0, c] + w1 * spread[n, 1, c]

        def plane_whole(x, carry):
            for c in range(3):
                below, above = halo_rows(c, x)
                dst[c, x + 1] = moved(c, x, below, above) + body_force(c, x)
            return carry

        def plane_rest(x, carry):
            for c in range(3):
                below, above = halo_rows(c, x)
                edge = jnp.where(is_first_y, below, jnp.where(is_last_y, above, 0.0))
                dst[c, x + 1] = dst[c, x + 1] + (body_force(c, x) + DIFFUSE * edge)
            return carry

        def store(k, low, high):
            if n == STEPS - 1:
                copy = pltpu.make_async_copy(
                    dst.at[:, pl.ds(1 + low, high - low)],
                    out_hbm.at[:, pl.ds(low, high - low)],
                    store_sem.at[k],
                )
                copy.start()
                stores.append(copy)

        lax.fori_loop(split, cx - 1, plane_whole, 0, unroll=UNROLL)
        if n == STEPS - 1:
            end_copies = gather_next(1, end_copies, end_g1, end_g2)
        plane_whole(cx - 1, 0)
        store(0, split, cx)
        plane_whole(0, 0)
        half = split // 2
        lax.fori_loop(1, half, plane_rest, 0, unroll=UNROLL)
        store(1, 0, half)
        lax.fori_loop(half, split, plane_rest, 0, unroll=UNROLL)
        store(2, half, split)

    for copy in end_copies:
        copy.wait_recv()
    home_x = pos_ref[0, tile] // cx
    home_y = pos_ref[1, tile] // cy
    block = end_g2[home_x, home_y]
    in_first = cross_ref[0, home_x * ny + home_y] == BLADES * tile
    state_ref[...] = jnp.where(in_first, block[0:BLADES], block[BLADES : 2 * BLADES])
    for copy in started:
        copy.wait_send()
    for copy in stores:
        copy.wait()


def per_device(
    velocity, inflow, azimuth, positions, crossings, lag_state, lag_rate, chord_len, twist_angle
):
    nx = lax.axis_size("gx")
    ny = lax.axis_size("gy")
    comps, cx, cy, nz = velocity.shape
    own, sections = lag_state.shape
    assert comps == 3 and own == BLADES and sections == nz
    f32 = jnp.float32
    grid = pltpu.VMEM((3, cx + 2, cy, nz), f32)
    dma = pltpu.SemaphoreType.DMA
    vmem = pl.BlockSpec(memory_space=pltpu.VMEM)
    smem = pl.BlockSpec(memory_space=pltpu.SMEM)
    hbm = pl.BlockSpec(memory_space=pl.ANY)
    return pl.pallas_call(
        functools.partial(farm_kernel, nx, ny),
        out_shape=(
            jax.ShapeDtypeStruct(velocity.shape, f32),
            jax.ShapeDtypeStruct(lag_state.shape, f32),
        ),
        in_specs=[hbm, vmem, smem, smem, smem, vmem, vmem, vmem, vmem],
        out_specs=(hbm, vmem),
        scratch_shapes=[
            grid,
            grid,
            grid,
            pltpu.VMEM((STEPS, 2, 3, cy, nz), f32),
            pltpu.VMEM((STEPS, 2, 3, cx, nz), f32),
            pltpu.VMEM((STEPS, 2, 3, cx, nz), f32),
            pltpu.VMEM((STEPS, 3, ROWS, nz), f32),
            pltpu.VMEM((STEPS, 2, 3, ROWS, nz), f32),
            pltpu.VMEM((STEPS, ENTRIES, cy, BLADES * nz), f32),
            pltpu.VMEM((STEPS, ENTRIES, nz, BLADES * nz), f32),
            pltpu.VMEM((STEPS, ENTRIES, 3, cy, nz), f32),
            pltpu.VMEM((ROWS, nz), f32),
            pltpu.VMEM((ny, ROWS, nz), f32),
            pltpu.VMEM((nx, ny, ROWS, nz), f32),
            pltpu.VMEM((ROWS, nz), f32),
            pltpu.VMEM((ny, ROWS, nz), f32),
            pltpu.VMEM((nx, ny, ROWS, nz), f32),
            dma,
            dma((CHUNKS,)),
            dma((STEPS, 2)),
            dma((STEPS, 2)),
            dma((STEPS, 2)),
            dma((STEPS, 2)),
            dma((STEPS, 2)),
            dma((STEPS, 2)),
            dma((2, ny)),
            dma((2, ny)),
            dma((2, nx)),
            dma((2, nx)),
        ],
        compiler_params=pltpu.CompilerParams(
            collective_id=0, has_side_effects=True, vmem_limit_bytes=60 * 1024 * 1024
        ),
        cost_estimate=pl.CostEstimate(
            flops=50_000_000, bytes_accessed=8 * velocity.size, transcendentals=500_000
        ),
    )(
        velocity,
        inflow,
        azimuth,
        positions.T,
        crossings.T,
        lag_state,
        lag_rate,
        chord_len.reshape(1, sections),
        twist_angle.reshape(1, sections),
    )


def solution(mesh):
    return jax.shard_map(
        per_device,
        mesh=mesh,
        in_specs=(
            P(None, "gx", "gy", None),
            P(None, "gy", None),
            P(),
            P(),
            P(),
            P(("gx", "gy"), None),
            P(("gx", "gy"), None),
            P(),
            P(),
        ),
        out_specs=(P(None, "gx", "gy", None), P(("gx", "gy"), None)),
        check_vma=False,
    )
```

```python
import functools
import math

import jax
import jax.numpy as jnp
from jax import lax
from jax.experimental import pallas as pl
from jax.experimental.pallas import tpu as pltpu
from jax.sharding import PartitionSpec as P

RADIUS = 12
HUB = 15
STEPS = 2
EPSILON = 2.0
SUPPORT = 3.0
TURN_RATE = 0.1
SPIN = 0.25
LIFT_SLOPE = 2.0 * math.pi
FORCE_SCALE = 0.15
ADVECT = 0.5
DIFFUSE = 0.05
PRECISE = lax.Precision.HIGHEST
MESH = pl.DeviceIdType.MESH
BLADES = 3
ENTRIES = 2
ROWS = 8
CHUNKS = 3
UNROLL = 4


def taper_const(distance):
    square = distance * distance
    term = max(1.0 - square / (SUPPORT * SUPPORT), 0.0)
    return math.exp(-square / EPSILON**2) * term * term / (EPSILON * math.sqrt(math.pi))


KERN_X = [taper_const(float(i)) for i in range(3)]


def taper_kernel(distance):
    square = distance * distance
    term = jnp.maximum(1.0 - square * (1.0 / (SUPPORT * SUPPORT)), 0.0)
    return (
        jnp.exp(square * (-1.0 / (EPSILON * EPSILON)))
        * (term * term)
        * (1.0 / (EPSILON * math.sqrt(math.pi)))
    )


def weight_x(offset):
    dist = jnp.abs(offset)
    return jnp.where(
        dist == 0,
        KERN_X[0],
        jnp.where(dist == 1, KERN_X[1], jnp.where(dist == 2, KERN_X[2], 0.0)),
    ).astype(jnp.float32)


def farm_kernel(
    nx,
    ny,
    vel_hbm,
    inflow_hbm,
    az_hbm,
    pos_hbm,
    cross_hbm,
    lag_hbm,
    rate_hbm,
    chord_hbm,
    twist_hbm,
    out_hbm,
    state_hbm,
    inflow_ref,
    az_ref,
    pos_ref,
    cross_ref,
    lag_ref,
    rate_ref,
    chord_ref,
    twist_ref,
    state_ref,
    small_sem,
    grid0,
    grid1,
    grid2,
    halo_x,
    halo_y,
    face_y,
    part_out,
    part_in,
    kern_y,
    kern_z,
    spread,
    lag_pack,
    lag_g1,
    lag_g2,
    end_pack,
    end_g1,
    end_g2,
    load_sem,
    store_sem,
    hx_send,
    hx_recv,
    hy_send,
    hy_recv,
    ps_send,
    ps_recv,
    gy_send,
    gy_recv,
    gx_send,
    gx_recv,
):
    grids = (grid0, grid1, grid2)
    _, cx2, cy, nz = grid0.shape
    cx = cx2 - 2
    split = cx * 3 // 4
    total_y = cy * ny
    gx = lax.axis_index("gx")
    gy = lax.axis_index("gy")
    tile = gx * ny + gy
    east = lax.rem(gx + 1, nx)
    west = lax.rem(gx + nx - 1, nx)
    up = lax.rem(gy + 1, ny)
    down = lax.rem(gy + ny - 1, ny)

    load = pltpu.make_async_copy(vel_hbm, grid0.at[:, pl.ds(1, cx)], load_sem)
    smalls = [
        pltpu.make_async_copy(source, target, small_sem.at[i])
        for i, (source, target) in enumerate(
            (
                (az_hbm, az_ref),
                (pos_hbm, pos_ref),
                (cross_hbm, cross_ref),
                (lag_hbm, lag_ref),
                (rate_hbm, rate_ref),
                (chord_hbm, chord_ref),
                (twist_hbm, twist_ref),
                (inflow_hbm, inflow_ref),
            )
        )
    ]
    for copy in smalls:
        copy.start()
    load.start()

    barrier = pltpu.get_barrier_semaphore()
    for d in range(1, ny):
        pl.semaphore_signal(
            barrier, inc=1, device_id={"gy": lax.rem(gy + d, ny)}, device_id_type=MESH
        )
    for d in range(1, nx):
        pl.semaphore_signal(
            barrier, inc=1, device_id={"gx": lax.rem(gx + d, nx)}, device_id_type=MESH
        )

    for copy in smalls:
        copy.wait()

    rotor, hub_x, load_x, shift_y, valid, az = [], [], [], [], [], []
    for e in range(ENTRIES):
        blade = cross_ref[BLADES * e, tile]
        r = jnp.where(blade >= 0, blade, 0) // BLADES
        rotor.append(jnp.where(blade >= 0, r, -1))
        valid.append(jnp.where(blade >= 0, 1.0, 0.0).astype(jnp.float32))
        hub_x.append(jnp.where(blade >= 0, pos_ref[0, r] - gx * cx, 2))
        load_x.append(jnp.clip(hub_x[e], 2, cx - 3))
        off = gy * cy - pos_ref[1, r] + total_y + total_y // 2
        shift_y.append(lax.rem(off, total_y) - total_y // 2)
        az.append(az_ref[r])

    def matches(other):
        found = []
        for f in range(ENTRIES):
            blade = cross_ref[BLADES * f, other]
            found.append(jnp.where(blade >= 0, jnp.where(blade >= 0, blade, 0) // BLADES, -2))
        return [
            [jnp.where(rotor[e] == found[f], 1.0, 0.0).astype(jnp.float32) for f in range(ENTRIES)]
            for e in range(ENTRIES)
        ]

    row = lax.broadcasted_iota(jnp.int32, (ROWS, nz), 0)
    first = row < BLADES
    lane8 = lax.broadcasted_iota(jnp.int32, (ROWS, nz), 1).astype(jnp.float32)
    radius = RADIUS * (lane8 + 0.5) / nz
    spin = jnp.where(first, row, row - BLADES).astype(jnp.float32) * (2.0 * math.pi / 3.0)
    base = jnp.where(first, az[0], az[1])
    mask_rows = []
    for other in (gx * ny + down, gx * ny + up):
        m = matches(other)
        mask_rows.append(
            (jnp.where(first, m[0][0], m[1][1]), jnp.where(first, m[0][1], m[1][0]))
        )
    cos_all, sin_all = [], []
    rows_y = lax.broadcasted_iota(jnp.int32, (cy, nz), 0)
    rows_z = lax.broadcasted_iota(jnp.int32, (nz, nz), 0).astype(jnp.float32) - HUB
    for n in range(STEPS):
        theta = base + TURN_RATE * n + spin
        cos_n, sin_n = jnp.cos(theta), jnp.sin(theta)
        cos_all.append(cos_n)
        sin_all.append(sin_n)
        rc, rs = radius * cos_n, radius * sin_n
        for e in range(ENTRIES):
            y_rel = (rows_y + shift_y[e]).astype(jnp.float32)
            for b in range(BLADES):
                i = BLADES * e + b
                kern_y[n, e, :, b * nz : (b + 1) * nz] = taper_kernel(y_rel - rs[i : i + 1]) * valid[e]
                kern_z[n, e, :, b * nz : (b + 1) * nz] = taper_kernel(rows_z - rc[i : i + 1])
    cos_t, sin_t = jnp.cos(twist_ref[...]), jnp.sin(twist_ref[...])
    chord = FORCE_SCALE * chord_ref[...]

    lag_pack[0:BLADES] = lag_ref[...]
    lag_pack[BLADES : 2 * BLADES] = rate_ref[...]
    lag_pack[2 * BLADES : ROWS] = jnp.zeros((ROWS - 2 * BLADES, nz), jnp.float32)

    pl.semaphore_wait(barrier, nx - 1 + ny - 1)

    started = []

    def send(src, dst, send_sem, recv_sem, axis, peer):
        copy = pltpu.make_async_remote_copy(
            src_ref=src,
            dst_ref=dst,
            send_sem=send_sem,
            recv_sem=recv_sem,
            device_id={axis: peer},
            device_id_type=MESH,
        )
        copy.start()
        started.append(copy)
        return copy

    def gather_start(k, pack, first_level):
        copies = [
            send(pack, first_level.at[gy], gy_send.at[k, d], gy_recv.at[k, d], "gy", lax.rem(gy + d, ny))
            for d in range(1, ny)
        ]
        first_level[gy] = pack[...]
        return copies

    def gather_next(k, copies, first_level, second_level):
        for copy in copies:
            copy.wait_recv()
        copies = [
            send(first_level, second_level.at[gx], gx_send.at[k, d], gx_recv.at[k, d], "gx", lax.rem(gx + d, nx))
            for d in range(1, nx)
        ]
        second_level[gx] = first_level[...]
        return copies

    lag_copies = gather_start(0, lag_pack, lag_g1)
    load.wait()

    lag = None
    rate = None
    zero_rows = jnp.zeros((ROWS - 2 * BLADES, nz), jnp.float32)
    lane = lax.broadcasted_iota(jnp.int32, (cy, nz), 1)
    row_c = lax.broadcasted_iota(jnp.int32, (cy, nz), 0)
    is_first_z, is_last_z = lane == 0, lane == nz - 1
    is_first_y, is_last_y = row_c == 0, row_c == cy - 1
    end_copies = None
    stores = []
    for n in range(STEPS):
        src, dst = grids[n], grids[n + 1]
        sampled = [[], [], []]
        for e in range(ENTRIES):
            field = None
            for i in range(-2, 3):
                term = KERN_X[abs(i)] * src[:, load_x[e] + 1 + i]
                field = term if field is None else field + term
            inner = jnp.dot(
                field.reshape(3 * cy, nz),
                kern_z[n, e],
                precision=PRECISE,
                preferred_element_type=jnp.float32,
            )
            for c in range(3):
                reduced = jnp.sum(inner[c * cy : (c + 1) * cy] * kern_y[n, e], axis=0, keepdims=True)
                sampled[c] += [reduced[:, b * nz : (b + 1) * nz] for b in range(BLADES)]
        for c in range(3):
            part_out[n, c] = jnp.concatenate(sampled[c] + [zero_rows], axis=0)
        part_copies = [
            send(part_out.at[n], part_in.at[n, 0], ps_send.at[n, 0], ps_recv.at[n, 0], "gy", up),
            send(part_out.at[n], part_in.at[n, 1], ps_send.at[n, 1], ps_recv.at[n, 1], "gy", down),
        ]
        halo_copies = [
            send(src.at[:, cx], halo_x.at[n, 0], hx_send.at[n, 0], hx_recv.at[n, 0], "gx", east),
            send(src.at[:, 1], halo_x.at[n, 1], hx_send.at[n, 1], hx_recv.at[n, 1], "gx", west),
        ]

        flat = src.reshape(3 * cx2 * cy, nz)
        for c in range(3):
            start = (c * cx2 + 1) * cy
            face_y[n, 0, c] = flat[pl.ds(start + cy - 1, cx, stride=cy), :]
            face_y[n, 1, c] = flat[pl.ds(start, cx, stride=cy), :]
        halo_copies += [
            send(face_y.at[n, 0], halo_y.at[n, 0], hy_send.at[n, 0], hy_recv.at[n, 0], "gy", up),
            send(face_y.at[n, 1], halo_y.at[n, 1], hy_send.at[n, 1], hy_recv.at[n, 1], "gy", down),
        ]
        if n == 0:
            lag_copies = gather_next(0, lag_copies, lag_g1, lag_g2)

        def halo_rows(c, x):
            return halo_y[n, 0, c, pl.ds(x, 1), :], halo_y[n, 1, c, pl.ds(x, 1), :]

        def moved(c, x, below, above):
            cur = src[c, x + 1]
            y_prev = jnp.where(is_first_y, below, pltpu.roll(cur, 1, 0))
            y_next = jnp.where(is_last_y, above, pltpu.roll(cur, cy - 1, 0))
            z_prev = jnp.where(is_first_z, 0.0, pltpu.roll(cur, 1, 1))
            z_next = jnp.where(is_last_z, cur, pltpu.roll(cur, nz - 1, 1))
            others = (src[c, x + 2] + (y_prev + y_next)) + (z_prev + z_next)
            return (
                (1.0 - ADVECT - 6.0 * DIFFUSE) * cur
                + (ADVECT + DIFFUSE) * src[c, x]
                + DIFFUSE * others
            )

        def plane_alone(x, carry):
            for c in range(3):
                dst[c, x + 1] = moved(c, x, 0.0, 0.0)
            return carry

        lax.fori_loop(1, split, plane_alone, 0, unroll=UNROLL)

        for copy in part_copies:
            copy.wait_recv()
        whole = []
        for c in range(3):
            total = part_out[n, c]
            for side in range(2):
                other = part_in[n, side, c]
                same, cross = mask_rows[side]
                swapped = jnp.where(first, pltpu.roll(other, ROWS - BLADES, 0), pltpu.roll(other, BLADES, 0))
                total = total + (same * other + cross * swapped)
            whole.append(total)
        if n == 0:
            for copy in lag_copies:
                copy.wait_recv()
            state_rows, rate_rows = [], []
            for e in range(ENTRIES):
                r = jnp.maximum(rotor[e], 0)
                block = lag_g2[r // ny, lax.rem(r, ny)]
                state_rows.append(block[0:BLADES])
                rate_rows.append(block[BLADES : 2 * BLADES])
            lag = jnp.concatenate(state_rows + [zero_rows], axis=0)
            rate = jnp.concatenate(rate_rows + [zero_rows], axis=0)
        cos_b, sin_b = cos_all[n], sin_all[n]
        axial = whole[0]
        tangential = SPIN * radius - (whole[1] * cos_b - whole[2] * sin_b)
        magnitude = jnp.sqrt(axial * axial + tangential * tangential + 1.0)
        lift_static = LIFT_SLOPE * (axial * cos_t - tangential * sin_t) / magnitude
        lag = lag + rate * (lift_static - lag)
        if n == STEPS - 1:
            end_pack[...] = lag
            end_copies = gather_start(1, end_pack, end_g1)
        lift = chord * lag * magnitude
        forces = (-lift * tangential, lift * axial * cos_b, -lift * axial * sin_b)
        for e in range(ENTRIES):
            weighted = []
            for c in range(3):
                weighted.append(
                    jnp.concatenate(
                        [
                            forces[c][BLADES * e + b : BLADES * e + b + 1]
                            * kern_y[n, e, :, b * nz : (b + 1) * nz]
                            for b in range(BLADES)
                        ],
                        axis=1,
                    )
                )
            pushed = lax.dot_general(
                jnp.concatenate(weighted, axis=0),
                kern_z[n, e],
                (((1,), (1,)), ((), ())),
                precision=PRECISE,
                preferred_element_type=jnp.float32,
            )
            spread[n, e] = pushed.reshape(3, cy, nz)
        for copy in halo_copies:
            copy.wait_recv()
        src[:, 0] = jnp.where(gx == 0, inflow_ref[...], halo_x[n, 0])
        src[:, cx + 1] = jnp.where(gx == nx - 1, src[:, cx], halo_x[n, 1])

        def body_force(c, x):
            w0, w1 = weight_x(x - hub_x[0]), weight_x(x - hub_x[1])
            return w0 * spread[n, 0, c] + w1 * spread[n, 1, c]

        def plane_whole(x, carry):
            for c in range(3):
                below, above = halo_rows(c, x)
                dst[c, x + 1] = moved(c, x, below, above) + body_force(c, x)
            return carry

        def plane_rest(x, carry):
            for c in range(3):
                below, above = halo_rows(c, x)
                edge = jnp.where(is_first_y, below, jnp.where(is_last_y, above, 0.0))
                dst[c, x + 1] = dst[c, x + 1] + (body_force(c, x) + DIFFUSE * edge)
            return carry

        def store(k, low, high):
            if n == STEPS - 1:
                copy = pltpu.make_async_copy(
                    dst.at[:, pl.ds(1 + low, high - low)],
                    out_hbm.at[:, pl.ds(low, high - low)],
                    store_sem.at[k],
                )
                copy.start()
                stores.append(copy)

        lax.fori_loop(split, cx - 1, plane_whole, 0, unroll=UNROLL)
        if n == STEPS - 1:
            end_copies = gather_next(1, end_copies, end_g1, end_g2)
        plane_whole(cx - 1, 0)
        store(0, split, cx)
        plane_whole(0, 0)
        half = split // 2
        lax.fori_loop(1, half, plane_rest, 0, unroll=UNROLL)
        store(1, 0, half)
        lax.fori_loop(half, split, plane_rest, 0, unroll=UNROLL)
        store(2, half, split)

    for copy in end_copies:
        copy.wait_recv()
    home_x = pos_ref[0, tile] // cx
    home_y = pos_ref[1, tile] // cy
    block = end_g2[home_x, home_y]
    in_first = cross_ref[0, home_x * ny + home_y] == BLADES * tile
    state_ref[...] = jnp.where(in_first, block[0:BLADES], block[BLADES : 2 * BLADES])
    last = pltpu.make_async_copy(state_ref, state_hbm, small_sem.at[8])
    last.start()
    for copy in started:
        copy.wait_send()
    last.wait()
    for copy in stores:
        copy.wait()


def per_device(
    velocity, inflow, azimuth, positions, crossings, lag_state, lag_rate, chord_len, twist_angle
):
    nx = lax.axis_size("gx")
    ny = lax.axis_size("gy")
    comps, cx, cy, nz = velocity.shape
    own, sections = lag_state.shape
    assert comps == 3 and own == BLADES and sections == nz
    f32 = jnp.float32
    grid = pltpu.VMEM((3, cx + 2, cy, nz), f32)
    dma = pltpu.SemaphoreType.DMA
    hbm = pl.BlockSpec(memory_space=pl.ANY)
    return pl.pallas_call(
        functools.partial(farm_kernel, nx, ny),
        out_shape=(
            jax.ShapeDtypeStruct(velocity.shape, f32),
            jax.ShapeDtypeStruct(lag_state.shape, f32),
        ),
        in_specs=[hbm] * 9,
        out_specs=(hbm, hbm),
        scratch_shapes=[
            pltpu.VMEM(inflow.shape, f32),
            pltpu.SMEM(azimuth.shape, f32),
            pltpu.SMEM(positions.shape[::-1], jnp.int32),
            pltpu.SMEM(crossings.shape[::-1], jnp.int32),
            pltpu.VMEM(lag_state.shape, f32),
            pltpu.VMEM(lag_state.shape, f32),
            pltpu.VMEM((1, sections), f32),
            pltpu.VMEM((1, sections), f32),
            pltpu.VMEM(lag_state.shape, f32),
            dma((9,)),
            grid,
            grid,
            grid,
            pltpu.VMEM((STEPS, 2, 3, cy, nz), f32),
            pltpu.VMEM((STEPS, 2, 3, cx, nz), f32),
            pltpu.VMEM((STEPS, 2, 3, cx, nz), f32),
            pltpu.VMEM((STEPS, 3, ROWS, nz), f32),
            pltpu.VMEM((STEPS, 2, 3, ROWS, nz), f32),
            pltpu.VMEM((STEPS, ENTRIES, cy, BLADES * nz), f32),
            pltpu.VMEM((STEPS, ENTRIES, nz, BLADES * nz), f32),
            pltpu.VMEM((STEPS, ENTRIES, 3, cy, nz), f32),
            pltpu.VMEM((ROWS, nz), f32),
            pltpu.VMEM((ny, ROWS, nz), f32),
            pltpu.VMEM((nx, ny, ROWS, nz), f32),
            pltpu.VMEM((ROWS, nz), f32),
            pltpu.VMEM((ny, ROWS, nz), f32),
            pltpu.VMEM((nx, ny, ROWS, nz), f32),
            dma,
            dma((CHUNKS,)),
            dma((STEPS, 2)),
            dma((STEPS, 2)),
            dma((STEPS, 2)),
            dma((STEPS, 2)),
            dma((STEPS, 2)),
            dma((STEPS, 2)),
            dma((2, ny)),
            dma((2, ny)),
            dma((2, nx)),
            dma((2, nx)),
        ],
        compiler_params=pltpu.CompilerParams(
            collective_id=0, has_side_effects=True, vmem_limit_bytes=60 * 1024 * 1024
        ),
        cost_estimate=pl.CostEstimate(
            flops=50_000_000, bytes_accessed=8 * velocity.size, transcendentals=500_000
        ),
    )(
        velocity,
        inflow,
        azimuth,
        positions.T,
        crossings.T,
        lag_state,
        lag_rate,
        chord_len.reshape(1, sections),
        twist_angle.reshape(1, sections),
    )


def solution(mesh):
    return jax.shard_map(
        per_device,
        mesh=mesh,
        in_specs=(
            P(None, "gx", "gy", None),
            P(None, "gy", None),
            P(),
            P(),
            P(),
            P(("gx", "gy"), None),
            P(("gx", "gy"), None),
            P(),
            P(),
        ),
        out_specs=(P(None, "gx", "gy", None), P(("gx", "gy"), None)),
        check_vma=False,
    )
```
